32 devices in a mesh: dp: 16 (over z, x, core), seq: 2 (over y).
Axes of the slice: x: 2, y: 2, z: 4, core: 2. Of those that a mesh axis runs over, the one named last changes fastest.
Arguments:
- hidden_in: bfloat16 [16, 1024, 1024], P('dp', 'seq'), may hold values from -6 to 6
- cond_in: bfloat16 [16, 1024], P('dp'), may hold values from -6 to 6
- ada_weight: bfloat16 [1024, 6144], P(('dp', 'seq')), may hold values from -0.1875 to 0.1875
- ada_bias: bfloat16 [6144], P(('dp', 'seq')), may hold values from -3 to 3
- qkv_weight: bfloat16 [1024, 3072], P(('dp', 'seq')), may hold values from -0.1875 to 0.1875
- qv_bias: bfloat16 [2048], P(('dp', 'seq')), may hold values from -3 to 3
- proj_weight: bfloat16 [1024, 1024], P(('dp', 'seq')), may hold values from -1 to 1
- proj_bias: bfloat16 [1024], P(('dp', 'seq')), may hold values from -3 to 3
- up_weight: bfloat16 [1024, 4096], P(('dp', 'seq')), may hold values from -0.1875 to 0.1875
- up_bias: bfloat16 [4096], P(('dp', 'seq')), may hold values from -3 to 3
- down_weight: bfloat16 [4096, 1024], P(('dp', 'seq')), may hold values from -0.09375 to 0.09375
- down_bias: bfloat16 [1024], P(('dp', 'seq')), may hold values from -3 to 3
- out_cot: bfloat16 [16, 1024, 1024], P('dp', 'seq'), may hold values from -6 to 6
Outputs:
- mixed_out: bfloat16 [16, 1024, 1024], P('dp', 'seq')
- grad_input: float32 [16, 1024, 1024], P('dp', 'seq')
- grad_cond: float32 [16, 1024], P('dp')
- grad_ada_weight: float32 [1024, 6144], P(('dp', 'seq'))
- grad_ada_bias: float32 [6144], P(('dp', 'seq'))
- grad_qkv_weight: float32 [1024, 3072], P(('dp', 'seq'))
- grad_qv_bias: float32 [2048], P(('dp', 'seq'))
- grad_proj_weight: float32 [1024, 1024], P(('dp', 'seq'))
- grad_proj_bias: float32 [1024], P(('dp', 'seq'))
- grad_up_weight: float32 [1024, 4096], P(('dp', 'seq'))
- grad_up_bias: float32 [4096], P(('dp', 'seq'))
- grad_down_weight: float32 [4096, 1024], P(('dp', 'seq'))
- grad_down_bias: float32 [1024], P(('dp', 'seq'))
The draws below stay inside these ranges and needn't reach their ends.
All inputs are finite; a program needn't handle non-finite values.
Results may differ from the reference program's by a relative error of at most 0.012.
The reference program's roundings to bfloat16 on the way count: a program that leaves them out, or rounds other values in their place, can miss the bound.
Values may be sent and summed in bfloat16 or wider, within the bound.
A program may use at most 256 MiB of HBM per device.

```python
import math
import jax
import jax.numpy as jnp
from jax import lax

D = 1024
H = 16
FF = 4096
C = 1024
L = 1024
LATENTS = 16


def block_levels(own_key, extent, cuts, smallest, high):
    factor_of, own = 1.0, jax.random.fold_in(own_key, 6)
    for dim, shards_of in cuts:
        heights = jnp.exp(jax.random.uniform(jax.random.fold_in(own, dim), (shards_of,), jnp.float32, smallest / len(cuts), high / len(cuts)))
        factor_of = factor_of * jnp.repeat(heights, extent[dim] // shards_of).reshape([-1 if axis == dim else 1 for axis in range(len(extent))])
    return factor_of


def scatter_about(stream_key, shape, deviation, limit, cuts=(), dtype=jnp.bfloat16):
    factor_of = block_levels(stream_key, shape, cuts, -0.22, 0.18) if cuts else 1.0
    drawn = jax.random.normal(stream_key, shape, jnp.float32) * deviation * factor_of
    return jnp.minimum(jnp.maximum(drawn, -limit), limit).astype(dtype)


def setup_inputs(seed: int = 0) -> dict:
    arg_keys = jax.random.split(jax.random.key(seed), 14)
    return {
        "hidden_in": scatter_about(arg_keys[0], (LATENTS, L, D), 1.0, 6.0, ((0, 16), (1, 2))),
        "cond_in": scatter_about(arg_keys[1], (LATENTS, C), 1.0, 6.0, ((0, 16),)),
        "ada_weight": scatter_about(arg_keys[2], (C, 6 * D), C ** -0.5, 0.1875, ((0, 32),)),
        "ada_bias": scatter_about(arg_keys[3], (6 * D,), 0.5, 3.0, ((0, 32),)),
        "qkv_weight": scatter_about(arg_keys[4], (D, 3 * D), D ** -0.5, 0.1875, ((0, 32),)),
        "qv_bias": scatter_about(arg_keys[5], (2 * D,), 0.5, 3.0, ((0, 32),)),
        "proj_weight": scatter_about(arg_keys[6], (D, D), (D // 32) ** -0.5, 1.0, ((0, 32),)),
        "proj_bias": scatter_about(arg_keys[7], (D,), 0.5, 3.0, ((0, 32),)),
        "up_weight": scatter_about(arg_keys[8], (D, FF), D ** -0.5, 0.1875, ((0, 32),)),
        "up_bias": scatter_about(arg_keys[9], (FF,), 0.5, 3.0, ((0, 32),)),
        "down_weight": scatter_about(arg_keys[10], (FF, D), FF ** -0.5, 0.09375, ((0, 32),)),
        "down_bias": scatter_about(arg_keys[11], (D,), 0.5, 3.0, ((0, 32),)),
        "out_cot": scatter_about(arg_keys[12], (LATENTS, L, D), 1.0, 6.0, ((0, 16), (1, 2))),
    }


@jax.custom_vjp
def low(v):
    return lax.optimization_barrier(v.astype(jnp.bfloat16)).astype(jnp.float32)

@jax.custom_vjp
def low_back(v):
    return v

def low_keep(v):
    return (low(v), None)

def low_pass(kept, grad):
    return (grad,)

def back_keep(v):
    return (v, None)

def back_low(kept, grad):
    return (low(grad),)
low.defvjp(low_keep, low_pass)
low_back.defvjp(back_keep, back_low)
exact_mode = lax.Precision.HIGHEST
norm_eps = 1e-06

def normalize(values):
    centre = values - lax.optimization_barrier(jnp.mean(values, axis=-1, keepdims=True))
    spread = lax.optimization_barrier(jnp.mean(centre * centre, axis=-1, keepdims=True))
    return centre * lax.rsqrt(spread + norm_eps)

def attend_one(qkv_one):
    queries = qkv_one[:, 0]
    keys_one = qkv_one[:, 1]
    values_one = qkv_one[:, 2]
    root = math.sqrt(queries.shape[-1])
    scores = low_back(jnp.einsum('qhd,khd->hqk', queries, keys_one, precision=exact_mode) / root)
    probs = low(jax.nn.softmax(scores, axis=-1))
    return jnp.einsum('hqk,khd->qhd', probs, values_one, precision=exact_mode)

def layer(latent, cond_vec, ada_w, ada_b, qkv_w, qv_b, proj_w, proj_b, up_w, up_b, down_w, down_b):
    count_lat, length, model_width = latent.shape
    cond_act = low(jax.nn.silu(cond_vec))
    modul = jnp.dot(cond_act, ada_w, precision=exact_mode) + ada_b
    modul = modul.reshape(count_lat, 6, 1, model_width)
    shift_att = modul[:, 0]
    scale_att = modul[:, 1]
    gate_att = modul[:, 2]
    shift_mlp = modul[:, 3]
    scale_mlp = modul[:, 4]
    gate_mlp = modul[:, 5]
    first_in = low(normalize(latent) * (1.0 + scale_att) + shift_att)
    zero_bias = jnp.zeros((model_width,), jnp.float32)
    qkv_bias = jnp.concatenate([qv_b[:model_width], zero_bias, qv_b[model_width:]])
    mixed = jnp.einsum('btd,de->bte', first_in, qkv_w, precision=exact_mode) + qkv_bias
    mixed = low(low_back(mixed))
    mixed = mixed.reshape(count_lat, length, 3, H, model_width // H)
    attended = lax.map(jax.checkpoint(attend_one), mixed)
    attended = low(low_back(attended.reshape(count_lat, length, model_width)))
    branch = low_back(jnp.einsum('btd,de->bte', attended, proj_w, precision=exact_mode) + proj_b)
    middle = latent + gate_att * branch
    second_in = low(normalize(middle) * (1.0 + scale_mlp) + shift_mlp)
    up_pre = low_back(jnp.einsum('btd,df->btf', second_in, up_w, precision=exact_mode) + up_b)
    act_low = low(jax.nn.gelu(up_pre, approximate=True))
    mlp_out = low_back(jnp.einsum('btf,fd->btd', act_low, down_w, precision=exact_mode) + down_b)
    return middle + gate_mlp * mlp_out

def reference(hidden_in, cond_in, ada_weight, ada_bias, qkv_weight, qv_bias, proj_weight, proj_bias, up_weight, up_bias, down_weight, down_bias, out_cot):
    params = tuple((item.astype(jnp.float32) for item in (ada_weight, ada_bias, qkv_weight, qv_bias, proj_weight, proj_bias, up_weight, up_bias, down_weight, down_bias)))
    group = math.gcd(LATENTS, max(1, 4096 // L))
    steps_count = LATENTS // group
    latent_all = hidden_in.astype(jnp.float32).reshape(steps_count, group, L, D)
    cond_all = cond_in.astype(jnp.float32).reshape(steps_count, group, C)
    cot_all = out_cot.astype(jnp.float32).reshape(steps_count, group, L, D)

    def one_group(totals, item):
        latent, cond_vec, cot_one = item
        result, pull = jax.vjp(layer, latent, cond_vec, *params)
        grads = pull(cot_one)
        totals = tuple((total + grad for total, grad in zip(totals, grads[2:])))
        return (totals, (result.astype(jnp.bfloat16), grads[0], grads[1]))
    start = tuple((jnp.zeros_like(item) for item in params))
    totals, (results, grad_latent, grad_condition) = lax.scan(one_group, start, (latent_all, cond_all, cot_all))
    return (results.reshape(LATENTS, L, D), grad_latent.reshape(LATENTS, L, D), grad_condition.reshape(LATENTS, C), totals[0], totals[1], totals[2], totals[3], totals[4], totals[5], totals[6], totals[7], totals[8], totals[9])
```

```python
import functools
import math

import jax
import jax.numpy as jnp
from jax import lax
from jax.experimental import pallas as pl
from jax.experimental.pallas import tpu as pltpu
from jax.sharding import PartitionSpec as P

H = 16


norm_eps = 1e-06
exact_mode = lax.Precision.HIGHEST


def normalize_rows(values):
    centre = values - jnp.mean(values, axis=-1, keepdims=True)
    inv_std = lax.rsqrt(jnp.mean(centre * centre, axis=-1, keepdims=True) + norm_eps)
    return (centre * inv_std, inv_std)


def norm_back(grad_norm, normed, inv_std):
    first_mean = jnp.mean(grad_norm, axis=-1, keepdims=True)
    second_mean = jnp.mean(grad_norm * normed, axis=-1, keepdims=True)
    return inv_std * (grad_norm - first_mean - normed * second_mean)


def gelu_tanh(inputs):
    return jax.nn.gelu(inputs, approximate=True)


NT = (((1,), (1,)), ((), ()))
TN = (((0,), (0,)), ((), ()))
LANES = 128


def mm(left, right, dims=None):
    if dims is None:
        return jnp.dot(left, right, preferred_element_type=jnp.float32)
    return lax.dot_general(left, right, dims, preferred_element_type=jnp.float32)


def head_masks(head_dim):
    lane = lax.broadcasted_iota(jnp.int32, (1, LANES), 1)
    return [lane // head_dim == one for one in range(LANES // head_dim)]


def attend_kernel(head_dim, block, qkv_ref, out_ref):
    masks = head_masks(head_dim)
    factor = jnp.bfloat16(1.0 / math.sqrt(head_dim))

    def step(index, carry):
        rows = pl.ds(pl.multiple_of(index * block, block), block)
        queries = qkv_ref[0, 0, rows, :] * factor
        output = jnp.zeros((block, LANES), jnp.float32)
        for mask in masks:
            own = jnp.where(mask, queries, jnp.zeros_like(queries))
            scores = mm(own, qkv_ref[0, 1], NT)
            expo = jnp.exp(scores - jnp.max(scores, axis=1, keepdims=True))
            inverse = 1.0 / jnp.sum(expo, axis=1, keepdims=True)
            probs_low = (expo * inverse).astype(jnp.bfloat16)
            output = jnp.where(mask, mm(probs_low, qkv_ref[0, 2]), output)
        out_ref[0, rows, :] = output.astype(jnp.bfloat16)
        return carry

    lax.fori_loop(0, qkv_ref.shape[2] // block, step, 0)


def attend_back_kernel(head_dim, block, qkv_ref, cot_ref, out_ref, keys_acc, values_acc):
    masks = head_masks(head_dim)
    factor = jnp.bfloat16(1.0 / math.sqrt(head_dim))
    keys_acc[...] = jnp.zeros_like(keys_acc)
    values_acc[...] = jnp.zeros_like(values_acc)

    def step(index, carry):
        rows = pl.ds(pl.multiple_of(index * block, block), block)
        queries = qkv_ref[0, 0, rows, :] * factor
        cot = cot_ref[0, rows, :]
        grad_queries = jnp.zeros((block, LANES), jnp.float32)
        for mask in masks:
            own = jnp.where(mask, queries, jnp.zeros_like(queries))
            own_cot = jnp.where(mask, cot, jnp.zeros_like(cot))
            scores = mm(qkv_ref[0, 1], own, NT)
            expo = jnp.exp(scores - jnp.max(scores, axis=0, keepdims=True))
            probs = expo * (1.0 / jnp.sum(expo, axis=0, keepdims=True))
            grad_probs = mm(qkv_ref[0, 2], own_cot, NT)
            inner = jnp.sum(probs * grad_probs, axis=0, keepdims=True)
            grad_scores = (probs * (grad_probs - inner)).astype(jnp.bfloat16)
            values_acc[...] += mm(probs.astype(jnp.bfloat16), own_cot)
            keys_acc[...] += mm(grad_scores, own)
            grad_queries = jnp.where(mask, mm(grad_scores, qkv_ref[0, 1], TN), grad_queries)
        grad_queries = grad_queries * (1.0 / math.sqrt(head_dim))
        out_ref[0, 0, rows, :] = grad_queries.astype(jnp.bfloat16)
        return carry

    lax.fori_loop(0, qkv_ref.shape[2] // block, step, 0)
    out_ref[0, 1] = keys_acc[...].astype(jnp.bfloat16)
    out_ref[0, 2] = values_acc[...].astype(jnp.bfloat16)


def attend(heads, head_dim):
    groups, _, length, width = heads.shape
    work = groups * width * length * length
    return pl.pallas_call(
        functools.partial(attend_kernel, head_dim, min(length, 256)),
        out_shape=jax.ShapeDtypeStruct((groups, length, width), jnp.bfloat16),
        grid=(groups, width // LANES),
        in_specs=[pl.BlockSpec((1, 3, length, LANES), lambda g, c: (g, 0, 0, c))],
        out_specs=pl.BlockSpec((1, length, LANES), lambda g, c: (g, 0, c)),
        compiler_params=pltpu.CompilerParams(vmem_limit_bytes=32 * 1024 * 1024),
        cost_estimate=pl.CostEstimate(
            flops=16 * work, bytes_accessed=8 * groups * length * width, transcendentals=0
        ),
    )(heads)


def attend_back(heads, grad_heads, head_dim):
    groups, _, length, width = heads.shape
    work = groups * width * length * length
    return pl.pallas_call(
        functools.partial(attend_back_kernel, head_dim, min(length, 256)),
        out_shape=jax.ShapeDtypeStruct(heads.shape, jnp.bfloat16),
        grid=(groups, width // LANES),
        in_specs=[
            pl.BlockSpec((1, 3, length, LANES), lambda g, c: (g, 0, 0, c)),
            pl.BlockSpec((1, length, LANES), lambda g, c: (g, 0, c)),
        ],
        out_specs=pl.BlockSpec((1, 3, length, LANES), lambda g, c: (g, 0, 0, c)),
        scratch_shapes=[pltpu.VMEM((length, LANES), jnp.float32)] * 2,
        compiler_params=pltpu.CompilerParams(vmem_limit_bytes=32 * 1024 * 1024),
        cost_estimate=pl.CostEstimate(
            flops=40 * work, bytes_accessed=14 * groups * length * width, transcendentals=0
        ),
    )(heads, grad_heads)


AXES = ("dp", "seq")
CORE_Y = (2, 1, 4, 8, 16)
CORE_X = (2, 4, 8, 1, 16)
CORE_Z = (2, 8, 4, 1, 16)


def axis_sizes():
    return lax.axis_size("dp"), lax.axis_size("seq")


def flat_index():
    return lax.axis_index("dp") * lax.axis_size("seq") + lax.axis_index("seq")


def swap(values, mask):
    dp_size, seq_size = axis_sizes()
    pairs = [(one, one ^ mask) for one in range(dp_size * seq_size)]
    return lax.ppermute(values, AXES, pairs)


def gather_small(values):
    dp_size, seq_size = axis_sizes()
    total = values[None]
    mask = 1
    while mask < dp_size * seq_size:
        other = swap(total, mask)
        upper = (flat_index() & mask) != 0
        total = jnp.concatenate(
            [jnp.where(upper, other, total), jnp.where(upper, total, other)], axis=0
        )
        mask *= 2
    return total


def sum_rows_by_latent(partial):
    dp_size, seq_size = axis_sizes()
    mask = dp_size * seq_size // 2
    total = partial
    while mask >= seq_size:
        half = total.shape[0] // 2
        bit = (flat_index() // mask) & 1
        sent = lax.dynamic_slice_in_dim(total, (1 - bit) * half, half, 0)
        kept = lax.dynamic_slice_in_dim(total, bit * half, half, 0)
        total = kept + swap(sent, mask)
        mask //= 2
    while mask >= 1:
        total = total + swap(total, mask)
        mask //= 2
    return total


def scatter_sum(grad, first_masks):
    dp_size, seq_size = axis_sizes()
    count = dp_size * seq_size
    rows, cols = grad.shape
    masks = []
    mask = count // 2
    while mask >= 1:
        masks.append(mask)
        mask //= 2
    order = [one for one in first_masks if one in masks]
    order += [one for one in masks if one not in order]
    total = grad.reshape([2] * len(masks) + [rows // count, cols])
    left = list(masks)
    for mask in order:
        axis = left.index(mask)
        left.pop(axis)
        bit = (flat_index() // mask) & 1
        sent = lax.dynamic_index_in_dim(total, 1 - bit, axis, keepdims=False)
        kept = lax.dynamic_index_in_dim(total, bit, axis, keepdims=False)
        total = kept.astype(jnp.float32) + swap(sent, mask).astype(jnp.float32)
        if left:
            total = total.astype(jnp.bfloat16)
    return total


def per_device(
    hidden_in,
    cond_in,
    ada_weight,
    ada_bias,
    qkv_weight,
    qv_bias,
    proj_weight,
    proj_bias,
    up_weight,
    up_bias,
    down_weight,
    down_bias,
    out_cot,
):
    groups, local_len, model_width = hidden_in.shape
    dp_size, seq_size = axis_sizes()
    count = dp_size * seq_size
    own_cond = ada_weight.shape[0]
    qkv_full = lax.all_gather(qkv_weight, AXES, axis=0, tiled=True)
    smalls = (ada_bias, qv_bias, proj_bias, up_bias, down_bias, cond_in.reshape(-1))
    packed = gather_small(jnp.concatenate(smalls))
    fulls = []
    offset = 0
    for one in smalls:
        width = one.shape[0]
        fulls.append(packed[:, offset : offset + width].reshape(-1))
        offset += width
    ada_bias_full, qv_bias_full, proj_bias_full, up_bias_full, down_bias_full, cond_copies = fulls
    cond_all = cond_copies.reshape(dp_size, seq_size, groups, -1)[:, 0]
    cond_all = cond_all.reshape(dp_size * groups, -1).astype(jnp.float32)
    cond_columns = lax.dynamic_slice_in_dim(cond_all, flat_index() * own_cond, own_cond, 1)
    cond_columns = jax.nn.silu(cond_columns).astype(jnp.bfloat16)
    proj_full = lax.all_gather(proj_weight, AXES, axis=0, tiled=True)
    up_full = lax.all_gather(up_weight, AXES, axis=0, tiled=True)
    down_full = lax.all_gather(down_weight, AXES, axis=0, tiled=True)
    row_count = groups * local_len
    cond_float = cond_in.astype(jnp.float32)
    modul = sum_rows_by_latent(
        jnp.dot(cond_columns, ada_weight, preferred_element_type=jnp.float32)
    ) + ada_bias_full.astype(jnp.float32)
    modul = modul.reshape(groups, 6, 1, model_width)
    shift_att = modul[:, 0]
    scale_att = modul[:, 1]
    gate_att = modul[:, 2]
    shift_mlp = modul[:, 3]
    scale_mlp = modul[:, 4]
    gate_mlp = modul[:, 5]
    source = hidden_in.astype(jnp.float32)
    normed_one, inv_one = normalize_rows(source)
    first_in = (normed_one * (1.0 + scale_att) + shift_att).astype(jnp.bfloat16)
    first_flat = first_in.reshape(row_count, model_width)
    qv_full = qv_bias_full.astype(jnp.float32)
    zero_bias = jnp.zeros((model_width,), jnp.float32)
    qkv_bias = jnp.concatenate([qv_full[:model_width], zero_bias, qv_full[model_width:]])
    mixed = jnp.dot(first_flat, qkv_full, preferred_element_type=jnp.float32) + qkv_bias
    mixed = mixed.astype(jnp.bfloat16).reshape(groups, local_len, 3, model_width)
    mixed = jnp.swapaxes(mixed, 1, 2)
    heads = lax.all_to_all(mixed, "seq", split_axis=3, concat_axis=2, tiled=True)
    head_dim = model_width // H
    attended = attend(heads, head_dim)
    back_tokens = lax.all_to_all(attended, "seq", split_axis=1, concat_axis=2, tiled=True)
    attended_flat = back_tokens.reshape(row_count, model_width)
    branch = jnp.dot(attended_flat, proj_full, preferred_element_type=jnp.float32)
    branch = branch + proj_bias_full.astype(jnp.float32)
    branch = branch.reshape(groups, local_len, model_width)
    middle = source + gate_att * branch
    normed_two, inv_two = normalize_rows(middle)
    second_in = (normed_two * (1.0 + scale_mlp) + shift_mlp).astype(jnp.bfloat16)
    second_flat = second_in.reshape(row_count, model_width)
    up_pre = jnp.dot(second_flat, up_full, preferred_element_type=jnp.float32) + up_bias_full.astype(
        jnp.float32
    )
    act_value, gelu_pull = jax.vjp(gelu_tanh, up_pre)
    act_low = act_value.astype(jnp.bfloat16)
    mlp_out = jnp.dot(act_low, down_full, preferred_element_type=jnp.float32) + down_bias_full.astype(
        jnp.float32
    )
    mlp_out = mlp_out.reshape(groups, local_len, model_width)
    result = (middle + gate_mlp * mlp_out).astype(jnp.bfloat16)
    grad_out = out_cot.astype(jnp.float32)
    grad_gate_mlp = jnp.sum(grad_out * mlp_out, axis=1)
    grad_mlp = (grad_out * gate_mlp).astype(jnp.bfloat16).reshape(row_count, model_width)
    grad_down_w = jnp.dot(act_low.T, grad_mlp, preferred_element_type=jnp.float32)
    own_down_w = scatter_sum(grad_down_w.astype(jnp.bfloat16), CORE_Y)
    grad_down_b = jnp.sum(grad_mlp.astype(jnp.float32), axis=0)
    grad_act = jnp.dot(grad_mlp, down_full.T, preferred_element_type=jnp.float32)
    grad_up = gelu_pull(grad_act)[0].astype(jnp.bfloat16)
    grad_up_w = jnp.dot(second_flat.T, grad_up, preferred_element_type=jnp.float32)
    own_up_w = scatter_sum(grad_up_w.astype(jnp.bfloat16), CORE_X)
    grad_up_b = jnp.sum(grad_up.astype(jnp.float32), axis=0)
    grad_second = jnp.dot(grad_up, up_full.T, preferred_element_type=jnp.float32).reshape(
        groups, local_len, model_width
    )
    grad_shift_mlp = jnp.sum(grad_second, axis=1)
    grad_scale_mlp = jnp.sum(grad_second * normed_two, axis=1)
    grad_middle = grad_out + norm_back(grad_second * (1.0 + scale_mlp), normed_two, inv_two)
    grad_gate_att = jnp.sum(grad_middle * branch, axis=1)
    grad_branch = (grad_middle * gate_att).astype(jnp.bfloat16).reshape(row_count, model_width)
    grad_proj_w = jnp.dot(attended_flat.T, grad_branch, preferred_element_type=jnp.float32)
    own_proj_w = scatter_sum(grad_proj_w.astype(jnp.bfloat16), CORE_Z)
    grad_proj_b = jnp.sum(grad_branch.astype(jnp.float32), axis=0)
    grad_attended = jnp.dot(grad_branch, proj_full.T, preferred_element_type=jnp.float32)
    grad_attended = grad_attended.astype(jnp.bfloat16).reshape(groups, local_len, model_width)
    grad_heads = lax.all_to_all(grad_attended, "seq", split_axis=2, concat_axis=1, tiled=True)
    grad_mixed = attend_back(heads, grad_heads, head_dim)
    grad_local = lax.all_to_all(grad_mixed, "seq", split_axis=2, concat_axis=3, tiled=True)
    grad_flat = jnp.swapaxes(grad_local, 1, 2).reshape(row_count, 3 * model_width)
    grad_qkv_w = jnp.dot(first_flat.T, grad_flat, preferred_element_type=jnp.float32)
    own_qkv_w = scatter_sum(grad_qkv_w.astype(jnp.bfloat16), CORE_Z)
    bias_total = jnp.sum(grad_flat.astype(jnp.float32), axis=0)
    grad_qv_b = jnp.concatenate([bias_total[:model_width], bias_total[2 * model_width :]])
    grad_first = jnp.dot(grad_flat, qkv_full.T, preferred_element_type=jnp.float32).reshape(
        groups, local_len, model_width
    )
    grad_shift_att = jnp.sum(grad_first, axis=1)
    grad_scale_att = jnp.sum(grad_first * normed_one, axis=1)
    grad_input = grad_middle + norm_back(grad_first * (1.0 + scale_att), normed_one, inv_one)
    grad_modul = jnp.stack(
        [
            grad_shift_att,
            grad_scale_att,
            grad_gate_att,
            grad_shift_mlp,
            grad_scale_mlp,
            grad_gate_mlp,
        ],
        axis=1,
    )
    grad_modul = grad_modul.reshape(groups, 6 * model_width)
    small_grads = (grad_qv_b, grad_proj_b, grad_up_b, grad_down_b, grad_modul.reshape(-1))
    gathered = gather_small(jnp.concatenate(small_grads))
    split_at = sum(one.shape[0] for one in small_grads[:-1])
    bias_sums = jnp.sum(gathered[:, :split_at], axis=0)
    modul_all = gathered[:, split_at:].reshape(dp_size, seq_size, groups, -1)
    modul_all = jnp.sum(modul_all, axis=1).reshape(dp_size * groups, -1)
    own_biases = []
    offset = 0
    for one in small_grads[:-1] + (jnp.sum(modul_all, axis=0),):
        width = one.shape[0]
        whole_bias = bias_sums[offset : offset + width] if offset < split_at else one
        offset += width
        own_width = width // count
        own_biases.append(
            lax.dynamic_slice_in_dim(whole_bias, flat_index() * own_width, own_width, 0)
        )
    cond_wide = cond_columns.astype(jnp.float32)
    own_ada_w = jnp.dot(cond_wide.T, modul_all, precision=exact_mode)
    cond_part = jnp.dot(modul_all, ada_weight.astype(jnp.float32).T, precision=exact_mode)
    cond_parts = gather_small(cond_part)
    cond_total = lax.dynamic_slice_in_dim(
        cond_parts, lax.axis_index("dp") * groups, groups, 1
    )
    cond_total = jnp.swapaxes(cond_total, 0, 1).reshape(groups, -1)
    silu_value, silu_pull = jax.vjp(jax.nn.silu, cond_float)
    grad_condition = silu_pull(cond_total)[0]
    return (
        result,
        grad_input,
        grad_condition,
        own_ada_w,
        own_biases[4],
        own_qkv_w,
        own_biases[0],
        own_proj_w,
        own_biases[1],
        own_up_w,
        own_biases[2],
        own_down_w,
        own_biases[3],
    )


def solution(mesh):
    placed = (
        P("dp", "seq", None),
        P("dp", None),
        P(("dp", "seq"), None),
        P(("dp", "seq")),
        P(("dp", "seq"), None),
        P(("dp", "seq")),
        P(("dp", "seq"), None),
        P(("dp", "seq")),
        P(("dp", "seq"), None),
        P(("dp", "seq")),
        P(("dp", "seq"), None),
        P(("dp", "seq")),
        P("dp", "seq", None),
    )
    return jax.shard_map(
        per_device,
        mesh=mesh,
        in_specs=placed,
        out_specs=(
            P("dp", "seq", None),
            P("dp", "seq", None),
            P("dp", None),
            P(("dp", "seq"), None),
            P(("dp", "seq")),
            P(("dp", "seq"), None),
            P(("dp", "seq")),
            P(("dp", "seq"), None),
            P(("dp", "seq")),
            P(("dp", "seq"), None),
            P(("dp", "seq")),
            P(("dp", "seq"), None),
            P(("dp", "seq")),
        ),
        check_vma=False,
    )
```

```python
import functools
import math

import jax
import jax.numpy as jnp
from jax import lax
from jax.experimental import pallas as pl
from jax.experimental.pallas import tpu as pltpu
from jax.sharding import PartitionSpec as P

H = 16


norm_eps = 1e-06
exact_mode = lax.Precision.HIGHEST


def normalize_rows(values):
    centre = values - jnp.mean(values, axis=-1, keepdims=True)
    inv_std = lax.rsqrt(jnp.mean(centre * centre, axis=-1, keepdims=True) + norm_eps)
    return (centre * inv_std, inv_std)


def norm_back(grad_norm, normed, inv_std):
    first_mean = jnp.mean(grad_norm, axis=-1, keepdims=True)
    second_mean = jnp.mean(grad_norm * normed, axis=-1, keepdims=True)
    return inv_std * (grad_norm - first_mean - normed * second_mean)


def gelu_tanh(inputs):
    return jax.nn.gelu(inputs, approximate=True)


NT = (((1,), (1,)), ((), ()))
TN = (((0,), (0,)), ((), ()))
LANES = 128


def mm(left, right, dims=None):
    if dims is None:
        return jnp.dot(left, right, preferred_element_type=jnp.float32)
    return lax.dot_general(left, right, dims, preferred_element_type=jnp.float32)


def head_masks(head_dim):
    lane = lax.broadcasted_iota(jnp.int32, (1, LANES), 1)
    return [lane // head_dim == one for one in range(LANES // head_dim)]


def attend_kernel(head_dim, block, qkv_ref, out_ref):
    masks = head_masks(head_dim)
    factor = jnp.bfloat16(1.0 / math.sqrt(head_dim))

    def step(index, carry):
        rows = pl.ds(pl.multiple_of(index * block, block), block)
        queries = qkv_ref[0, 0, rows, :] * factor
        output = jnp.zeros((block, LANES), jnp.float32)
        for mask in masks:
            own = jnp.where(mask, queries, jnp.zeros_like(queries))
            scores = mm(own, qkv_ref[0, 1], NT)
            expo = jnp.exp(scores - jnp.max(scores, axis=1, keepdims=True))
            inverse = 1.0 / jnp.sum(expo, axis=1, keepdims=True)
            probs_low = (expo * inverse).astype(jnp.bfloat16)
            output = jnp.where(mask, mm(probs_low, qkv_ref[0, 2]), output)
        out_ref[0, rows, :] = output.astype(jnp.bfloat16)
        return carry

    lax.fori_loop(0, qkv_ref.shape[2] // block, step, 0)


def attend_back_kernel(head_dim, block, qkv_ref, cot_ref, out_ref, keys_acc, values_acc):
    masks = head_masks(head_dim)
    factor = jnp.bfloat16(1.0 / math.sqrt(head_dim))
    keys_acc[...] = jnp.zeros_like(keys_acc)
    values_acc[...] = jnp.zeros_like(values_acc)

    def step(index, carry):
        rows = pl.ds(pl.multiple_of(index * block, block), block)
        queries = qkv_ref[0, 0, rows, :] * factor
        cot = cot_ref[0, rows, :]
        grad_queries = jnp.zeros((block, LANES), jnp.float32)
        for mask in masks:
            own = jnp.where(mask, queries, jnp.zeros_like(queries))
            own_cot = jnp.where(mask, cot, jnp.zeros_like(cot))
            scores = mm(qkv_ref[0, 1], own, NT)
            expo = jnp.exp(scores - jnp.max(scores, axis=0, keepdims=True))
            probs = expo * (1.0 / jnp.sum(expo, axis=0, keepdims=True))
            grad_probs = mm(qkv_ref[0, 2], own_cot, NT)
            inner = jnp.sum(probs * grad_probs, axis=0, keepdims=True)
            grad_scores = (probs * (grad_probs - inner)).astype(jnp.bfloat16)
            values_acc[...] += mm(probs.astype(jnp.bfloat16), own_cot)
            keys_acc[...] += mm(grad_scores, own)
            grad_queries = jnp.where(mask, mm(grad_scores, qkv_ref[0, 1], TN), grad_queries)
        grad_queries = grad_queries * (1.0 / math.sqrt(head_dim))
        out_ref[0, 0, rows, :] = grad_queries.astype(jnp.bfloat16)
        return carry

    lax.fori_loop(0, qkv_ref.shape[2] // block, step, 0)
    out_ref[0, 1] = keys_acc[...].astype(jnp.bfloat16)
    out_ref[0, 2] = values_acc[...].astype(jnp.bfloat16)


def attend(heads, head_dim):
    groups, _, length, width = heads.shape
    work = groups * width * length * length
    return pl.pallas_call(
        functools.partial(attend_kernel, head_dim, min(length, 256)),
        out_shape=jax.ShapeDtypeStruct((groups, length, width), jnp.bfloat16),
        grid=(groups, width // LANES),
        in_specs=[pl.BlockSpec((1, 3, length, LANES), lambda g, c: (g, 0, 0, c))],
        out_specs=pl.BlockSpec((1, length, LANES), lambda g, c: (g, 0, c)),
        compiler_params=pltpu.CompilerParams(vmem_limit_bytes=32 * 1024 * 1024),
        cost_estimate=pl.CostEstimate(
            flops=16 * work, bytes_accessed=8 * groups * length * width, transcendentals=0
        ),
    )(heads)


def attend_back(heads, grad_heads, head_dim):
    groups, _, length, width = heads.shape
    work = groups * width * length * length
    return pl.pallas_call(
        functools.partial(attend_back_kernel, head_dim, min(length, 256)),
        out_shape=jax.ShapeDtypeStruct(heads.shape, jnp.bfloat16),
        grid=(groups, width // LANES),
        in_specs=[
            pl.BlockSpec((1, 3, length, LANES), lambda g, c: (g, 0, 0, c)),
            pl.BlockSpec((1, length, LANES), lambda g, c: (g, 0, c)),
        ],
        out_specs=pl.BlockSpec((1, 3, length, LANES), lambda g, c: (g, 0, 0, c)),
        scratch_shapes=[pltpu.VMEM((length, LANES), jnp.float32)] * 2,
        compiler_params=pltpu.CompilerParams(vmem_limit_bytes=32 * 1024 * 1024),
        cost_estimate=pl.CostEstimate(
            flops=40 * work, bytes_accessed=14 * groups * length * width, transcendentals=0
        ),
    )(heads, grad_heads)


AXES = ("dp", "seq")
CORE_Y = (2, 1, 4, 8, 16)
CORE_X = (2, 4, 8, 1, 16)
CORE_Z = (2, 8, 4, 1, 16)


def axis_sizes():
    return lax.axis_size("dp"), lax.axis_size("seq")


def flat_index():
    return lax.axis_index("dp") * lax.axis_size("seq") + lax.axis_index("seq")


def swap(values, mask):
    dp_size, seq_size = axis_sizes()
    pairs = [(one, one ^ mask) for one in range(dp_size * seq_size)]
    return lax.ppermute(values, AXES, pairs)


def gather_small(values):
    dp_size, seq_size = axis_sizes()
    total = values[None]
    mask = 1
    while mask < dp_size * seq_size:
        other = swap(total, mask)
        upper = (flat_index() & mask) != 0
        total = jnp.concatenate(
            [jnp.where(upper, other, total), jnp.where(upper, total, other)], axis=0
        )
        mask *= 2
    return total


def sum_rows_by_latent(partial):
    dp_size, seq_size = axis_sizes()
    mask = dp_size * seq_size // 2
    total = partial
    while mask >= seq_size:
        half = total.shape[0] // 2
        bit = (flat_index() // mask) & 1
        sent = lax.dynamic_slice_in_dim(total, (1 - bit) * half, half, 0)
        kept = lax.dynamic_slice_in_dim(total, bit * half, half, 0)
        total = kept + swap(sent, mask)
        mask //= 2
    while mask >= 1:
        total = total + swap(total, mask)
        mask //= 2
    return total


def scatter_sum(grad, first_masks):
    dp_size, seq_size = axis_sizes()
    count = dp_size * seq_size
    rows, cols = grad.shape
    masks = []
    mask = count // 2
    while mask >= 1:
        masks.append(mask)
        mask //= 2
    order = [one for one in first_masks if one in masks]
    order += [one for one in masks if one not in order]
    total = grad.reshape([2] * len(masks) + [rows // count, cols])
    left = list(masks)
    for mask in order:
        axis = left.index(mask)
        left.pop(axis)
        bit = (flat_index() // mask) & 1
        sent = lax.dynamic_index_in_dim(total, 1 - bit, axis, keepdims=False)
        kept = lax.dynamic_index_in_dim(total, bit, axis, keepdims=False)
        total = kept.astype(jnp.float32) + swap(sent, mask).astype(jnp.float32)
        if left:
            total = total.astype(jnp.bfloat16)
    return total


def per_device(
    hidden_in,
    cond_in,
    ada_weight,
    ada_bias,
    qkv_weight,
    qv_bias,
    proj_weight,
    proj_bias,
    up_weight,
    up_bias,
    down_weight,
    down_bias,
    out_cot,
):
    groups, local_len, model_width = hidden_in.shape
    dp_size, seq_size = axis_sizes()
    count = dp_size * seq_size
    own_cond = ada_weight.shape[0]
    qkv_full = lax.all_gather(qkv_weight, AXES, axis=0, tiled=True)
    smalls = (ada_bias, qv_bias, proj_bias, up_bias, down_bias, cond_in.reshape(-1))
    packed = gather_small(jnp.concatenate(smalls))
    fulls = []
    offset = 0
    for one in smalls:
        width = one.shape[0]
        fulls.append(packed[:, offset : offset + width].reshape(-1))
        offset += width
    ada_bias_full, qv_bias_full, proj_bias_full, up_bias_full, down_bias_full, cond_copies = fulls
    cond_all = cond_copies.reshape(dp_size, seq_size, groups, -1)[:, 0]
    cond_all = cond_all.reshape(dp_size * groups, -1).astype(jnp.float32)
    cond_columns = lax.dynamic_slice_in_dim(cond_all, flat_index() * own_cond, own_cond, 1)
    cond_columns = jax.nn.silu(cond_columns).astype(jnp.bfloat16)
    proj_up = jnp.concatenate([proj_weight, up_weight], axis=1)
    proj_up_full = lax.all_gather(proj_up, AXES, axis=0, tiled=True)
    proj_full = proj_up_full[:, :model_width]
    up_full = proj_up_full[:, model_width:]
    down_full = lax.all_gather(down_weight, AXES, axis=0, tiled=True)
    row_count = groups * local_len
    cond_float = cond_in.astype(jnp.float32)
    modul = sum_rows_by_latent(
        jnp.dot(cond_columns, ada_weight, preferred_element_type=jnp.float32)
    ) + ada_bias_full.astype(jnp.float32)
    modul = modul.reshape(groups, 6, 1, model_width)
    shift_att = modul[:, 0]
    scale_att = modul[:, 1]
    gate_att = modul[:, 2]
    shift_mlp = modul[:, 3]
    scale_mlp = modul[:, 4]
    gate_mlp = modul[:, 5]
    source = hidden_in.astype(jnp.float32)
    normed_one, inv_one = normalize_rows(source)
    first_in = (normed_one * (1.0 + scale_att) + shift_att).astype(jnp.bfloat16)
    first_flat = first_in.reshape(row_count, model_width)
    qv_full = qv_bias_full.astype(jnp.float32)
    zero_bias = jnp.zeros((model_width,), jnp.float32)
    qkv_bias = jnp.concatenate([qv_full[:model_width], zero_bias, qv_full[model_width:]])
    mixed = jnp.dot(first_flat, qkv_full, preferred_element_type=jnp.float32) + qkv_bias
    mixed = mixed.astype(jnp.bfloat16).reshape(groups, local_len, 3, model_width)
    mixed = jnp.swapaxes(mixed, 1, 2)
    heads = lax.all_to_all(mixed, "seq", split_axis=3, concat_axis=2, tiled=True)
    head_dim = model_width // H
    attended = attend(heads, head_dim)
    back_tokens = lax.all_to_all(attended, "seq", split_axis=1, concat_axis=2, tiled=True)
    attended_flat = back_tokens.reshape(row_count, model_width)
    branch = jnp.dot(attended_flat, proj_full, preferred_element_type=jnp.float32)
    branch = branch + proj_bias_full.astype(jnp.float32)
    branch = branch.reshape(groups, local_len, model_width)
    middle = source + gate_att * branch
    normed_two, inv_two = normalize_rows(middle)
    second_in = (normed_two * (1.0 + scale_mlp) + shift_mlp).astype(jnp.bfloat16)
    second_flat = second_in.reshape(row_count, model_width)
    up_pre = jnp.dot(second_flat, up_full, preferred_element_type=jnp.float32) + up_bias_full.astype(
        jnp.float32
    )
    act_value, gelu_pull = jax.vjp(gelu_tanh, up_pre)
    act_low = act_value.astype(jnp.bfloat16)
    mlp_out = jnp.dot(act_low, down_full, preferred_element_type=jnp.float32) + down_bias_full.astype(
        jnp.float32
    )
    mlp_out = mlp_out.reshape(groups, local_len, model_width)
    result = (middle + gate_mlp * mlp_out).astype(jnp.bfloat16)
    grad_out = out_cot.astype(jnp.float32)
    grad_gate_mlp = jnp.sum(grad_out * mlp_out, axis=1)
    grad_mlp = (grad_out * gate_mlp).astype(jnp.bfloat16).reshape(row_count, model_width)
    grad_down_w = jnp.dot(act_low.T, grad_mlp, preferred_element_type=jnp.float32)
    own_down_w = scatter_sum(grad_down_w.astype(jnp.bfloat16), CORE_Y)
    grad_down_b = jnp.sum(grad_mlp.astype(jnp.float32), axis=0)
    grad_act = jnp.dot(grad_mlp, down_full.T, preferred_element_type=jnp.float32)
    grad_up = gelu_pull(grad_act)[0].astype(jnp.bfloat16)
    grad_up_w = jnp.dot(second_flat.T, grad_up, preferred_element_type=jnp.float32)
    own_up_w = scatter_sum(grad_up_w.astype(jnp.bfloat16), CORE_X)
    grad_up_b = jnp.sum(grad_up.astype(jnp.float32), axis=0)
    grad_second = jnp.dot(grad_up, up_full.T, preferred_element_type=jnp.float32).reshape(
        groups, local_len, model_width
    )
    grad_shift_mlp = jnp.sum(grad_second, axis=1)
    grad_scale_mlp = jnp.sum(grad_second * normed_two, axis=1)
    grad_middle = grad_out + norm_back(grad_second * (1.0 + scale_mlp), normed_two, inv_two)
    grad_gate_att = jnp.sum(grad_middle * branch, axis=1)
    grad_branch = (grad_middle * gate_att).astype(jnp.bfloat16).reshape(row_count, model_width)
    grad_proj_w = jnp.dot(attended_flat.T, grad_branch, preferred_element_type=jnp.float32)
    own_proj_w = scatter_sum(grad_proj_w.astype(jnp.bfloat16), CORE_Z)
    grad_proj_b = jnp.sum(grad_branch.astype(jnp.float32), axis=0)
    grad_attended = jnp.dot(grad_branch, proj_full.T, preferred_element_type=jnp.float32)
    grad_attended = grad_attended.astype(jnp.bfloat16).reshape(groups, local_len, model_width)
    grad_heads = lax.all_to_all(grad_attended, "seq", split_axis=2, concat_axis=1, tiled=True)
    grad_mixed = attend_back(heads, grad_heads, head_dim)
    grad_local = lax.all_to_all(grad_mixed, "seq", split_axis=2, concat_axis=3, tiled=True)
    grad_flat = jnp.swapaxes(grad_local, 1, 2).reshape(row_count, 3 * model_width)
    grad_qkv_w = jnp.dot(first_flat.T, grad_flat, preferred_element_type=jnp.float32)
    own_qkv_w = scatter_sum(grad_qkv_w.astype(jnp.bfloat16), CORE_Z)
    bias_total = jnp.sum(grad_flat.astype(jnp.float32), axis=0)
    grad_qv_b = jnp.concatenate([bias_total[:model_width], bias_total[2 * model_width :]])
    grad_first = jnp.dot(grad_flat, qkv_full.T, preferred_element_type=jnp.float32).reshape(
        groups, local_len, model_width
    )
    grad_shift_att = jnp.sum(grad_first, axis=1)
    grad_scale_att = jnp.sum(grad_first * normed_one, axis=1)
    grad_input = grad_middle + norm_back(grad_first * (1.0 + scale_att), normed_one, inv_one)
    grad_modul = jnp.stack(
        [
            grad_shift_att,
            grad_scale_att,
            grad_gate_att,
            grad_shift_mlp,
            grad_scale_mlp,
            grad_gate_mlp,
        ],
        axis=1,
    )
    grad_modul = grad_modul.reshape(groups, 6 * model_width)
    small_grads = (grad_qv_b, grad_proj_b, grad_up_b, grad_down_b, grad_modul.reshape(-1))
    gathered = gather_small(jnp.concatenate(small_grads))
    split_at = sum(one.shape[0] for one in small_grads[:-1])
    bias_sums = jnp.sum(gathered[:, :split_at], axis=0)
    modul_all = gathered[:, split_at:].reshape(dp_size, seq_size, groups, -1)
    modul_all = jnp.sum(modul_all, axis=1).reshape(dp_size * groups, -1)
    own_biases = []
    offset = 0
    for one in small_grads[:-1] + (jnp.sum(modul_all, axis=0),):
        width = one.shape[0]
        whole_bias = bias_sums[offset : offset + width] if offset < split_at else one
        offset += width
        own_width = width // count
        own_biases.append(
            lax.dynamic_slice_in_dim(whole_bias, flat_index() * own_width, own_width, 0)
        )
    cond_wide = cond_columns.astype(jnp.float32)
    own_ada_w = jnp.dot(cond_wide.T, modul_all, precision=exact_mode)
    cond_part = jnp.dot(modul_all, ada_weight.astype(jnp.float32).T, precision=exact_mode)
    cond_parts = gather_small(cond_part)
    cond_total = lax.dynamic_slice_in_dim(
        cond_parts, lax.axis_index("dp") * groups, groups, 1
    )
    cond_total = jnp.swapaxes(cond_total, 0, 1).reshape(groups, -1)
    silu_value, silu_pull = jax.vjp(jax.nn.silu, cond_float)
    grad_condition = silu_pull(cond_total)[0]
    return (
        result,
        grad_input,
        grad_condition,
        own_ada_w,
        own_biases[4],
        own_qkv_w,
        own_biases[0],
        own_proj_w,
        own_biases[1],
        own_up_w,
        own_biases[2],
        own_down_w,
        own_biases[3],
    )


def solution(mesh):
    placed = (
        P("dp", "seq", None),
        P("dp", None),
        P(("dp", "seq"), None),
        P(("dp", "seq")),
        P(("dp", "seq"), None),
        P(("dp", "seq")),
        P(("dp", "seq"), None),
        P(("dp", "seq")),
        P(("dp", "seq"), None),
        P(("dp", "seq")),
        P(("dp", "seq"), None),
        P(("dp", "seq")),
        P("dp", "seq", None),
    )
    return jax.shard_map(
        per_device,
        mesh=mesh,
        in_specs=placed,
        out_specs=(
            P("dp", "seq", None),
            P("dp", "seq", None),
            P("dp", None),
            P(("dp", "seq"), None),
            P(("dp", "seq")),
            P(("dp", "seq"), None),
            P(("dp", "seq")),
            P(("dp", "seq"), None),
            P(("dp", "seq")),
            P(("dp", "seq"), None),
            P(("dp", "seq")),
            P(("dp", "seq"), None),
            P(("dp", "seq")),
        ),
        check_vma=False,
    )
```
